256 devices in a mesh: rep: 32 (over z, y_hi, core), tp: 8 (over x, y_lo).
Axes of the slice: x: 4, y: 4 (y_hi: 2, y_lo: 2; y = y_hi * 2 + y_lo), z: 8, core: 2. Of those that a mesh axis runs over, the one named last changes fastest.
Arguments:
- prompt: bfloat16 [32768, 8192], P('rep', 'tp'), may hold values from -6 to 6
- norm_gain: float32 [8192], replicated, may hold values from 0.1 to 1.9
- kv_weight: bfloat16 [2, 8192, 1024], P(None, None, 'tp'), may hold values from -0.0625 to 0.0625
- kv_bias: bfloat16 [2, 1024], P(None, 'tp'), may hold values from -6 to 6
- page_dest: int32 [4096, 1], P('rep'), may hold values from 0 to 31; in each aligned block of 128 rows (0 to 127, 128 to 255, ...) at most 8 rows name the same one
- page_row: int32 [4096], P('rep'), may hold values from 0 to 15
- page_offset: int32 [4096], P('rep'), may hold values from 0 to 32760
- queries: bfloat16 [512, 8192], P('rep', 'tp'), as said below
- cache_keys: bfloat16 [512, 512, 1024], P('rep', None, 'tp'), as said below
- cache_values: bfloat16 [512, 512, 1024], P('rep', None, 'tp'), may hold values from -6 to 6
- lengths: int32 [512], P('rep'), may hold values from 16 to 512, as said below
Outputs:
- attended: bfloat16 [512, 8192], P('rep', 'tp')
The draws below stay inside these ranges and needn't reach their ends.
Inputs may be any that keep to these rules, and one draw needn't show every extreme that they name: `page_dest`: among the pages of one replica index (aligned blocks of 128 pages) no replica is named more than 8 times; some replica is named exactly 8 times. `lengths`: some row's length is exactly 512. `queries`: entries of order one to some tens. `cache_keys`: entries of order one.
All inputs are finite; a program needn't handle non-finite values.
Results may differ from the reference program's by a relative error of at most 0.018.
Values may be sent and summed in bfloat16 or wider, within the bound.
No kernel may reach another device: no remote copies, remote signals or barrier semaphores. Data moves between devices by JAX's collectives and lax.ppermute only.
A program may use at most 128 MiB of HBM per device.

```python
import math
import jax
import jax.numpy as jnp
import numpy as np
from jax import lax

D = 8192
Q_HEADS = 64
KV_HEADS = 8
HEAD_DIM = 128
TOK_DEV = 1024
PAGE = 8
PROMPT = 32768
ROWS_DEV = 16
CONTEXT = 512
MOST = 8
REPLICAS = 32
SPAN = 32768
ROWS = 512
N_REP = 32


def shared_keys(key):
    return jax.random.normal(key, (ROWS, CONTEXT, KV_HEADS * HEAD_DIM), jnp.float32)


def draw_cache_keys(key, part):
    base_keys = shared_keys(key)
    return base_keys.astype(jnp.bfloat16)


def draw_queries(key, part):
    key = jax.random.fold_in(key, 5)
    first_key = jax.random.fold_in(key, 0)
    drawn_queries = 2.0 * jax.random.normal(first_key, (ROWS, Q_HEADS * HEAD_DIM), jnp.float32)
    return drawn_queries.astype(jnp.bfloat16)


def draw_lengths(key, part):
    key = jax.random.fold_in(key, 7)
    first_key, second_key, third_key = jax.random.split(key, 3)
    group_count = ROWS // ROWS_DEV
    factor = jax.random.randint(first_key, (group_count, 1), 1, 5)
    raw_lengths = jax.random.randint(second_key, (group_count, ROWS_DEV), 4, CONTEXT // 4 + 1) * factor
    lengths_all = jnp.clip(raw_lengths, 16, CONTEXT).reshape(-1)
    position_pick = jax.random.randint(third_key, (), 0, ROWS)
    return lengths_all.at[position_pick].set(CONTEXT).astype(jnp.int32)


def set_ends(drawn, rng, least, top_value):
    dims = drawn.shape
    place = [jax.random.randint(jax.random.fold_in(rng, axis), (), 0, dims[axis]) for axis in range(len(dims))]
    drawn = drawn.at[tuple(place)].set(least)
    longest = dims.index(max(dims))
    place[longest] = (place[longest] + 1) % dims[longest]
    return drawn.at[tuple(place)].set(top_value)


def steps_of(rng, dims, cuts, low, largest):
    loudness, own = 1.0, jax.random.fold_in(rng, 6)
    for position, shards_of in cuts:
        steps = jnp.exp(jax.random.uniform(jax.random.fold_in(own, position), (shards_of,), jnp.float32, low / len(cuts), largest / len(cuts)))
        loudness = loudness * jnp.repeat(steps, dims[position] // shards_of).reshape([-1 if axis == position else 1 for axis in range(len(dims))])
    return loudness


def assign_block(own_key, own, number, rows, number_of, top, limit, skew):
    order = jax.random.permutation(own_key, number_of)
    heavy_load, ordinary = portions_of(number_of, rows * top, limit, skew, True), portions_of(number_of, rows * top, limit, skew, False)
    places = jnp.arange(number_of)

    def named(sizes, turn):
        used = int((sizes > 0).sum())
        fixed = max(1, used // 4)
        passed = fixed + (places - fixed + turn * (used - fixed)) % max(1, number_of - fixed)
        return jnp.zeros((number_of,), jnp.int32).at[order[jnp.where(places < fixed, places, passed)]].set(jnp.asarray(sizes, jnp.int32))

    sizes = jnp.where(number % 4 == 0, named(heavy_load, number // 4), named(ordinary, number - number // 4 - 1))
    mixed = jax.random.permutation(jax.random.fold_in(own, 3), number_of)
    source_of, taker = mixed[0:number_of // 2 * 2:2], mixed[1:number_of // 2 * 2:2]
    margin = jnp.minimum(sizes[source_of] - 1, limit - sizes[taker]) // 2
    margin = jnp.where((source_of == order[0]) | (taker == order[0]) | (sizes[taker] == 0), 0, jnp.maximum(margin, 0))
    passed = jax.random.randint(jax.random.fold_in(own, 4), (number_of // 2,), 0, 1 << 20) % (margin + 1)
    sizes = sizes.at[source_of].add(-passed).at[taker].add(passed)
    labels = jnp.searchsorted(jnp.cumsum(sizes), jnp.arange(rows * top), side="right").astype(jnp.int32)
    table = labels.reshape(top, rows).T
    table = table[jax.random.permutation(jax.random.fold_in(own, 1), rows)]
    turn = jax.random.randint(jax.random.fold_in(own, 2), (rows, 1), 0, top)
    return jnp.take_along_axis(table, (jnp.arange(top)[None, :] + turn) % top, axis=1)


def portions_of(count, total, bound, lean, full):
    portions = [(1 << 20) // math.isqrt(standing ** lean) + 1 for standing in range(1, count + 1)]
    largest = bound if full else min(bound, max(-(-total // count), total * portions[0] // sum(portions)))
    least = 1 if total - largest >= count - 1 else 0
    given, rest = [largest] + [least] * (count - 1), total - largest - least * (count - 1)
    while rest > 0:
        free = [i for i in range(1, count) if given[i] < largest] or [i for i in range(1, count) if given[i] < bound]
        mass, budget = sum([portions[i] for i in free]), rest
        for i in free:
            more = min(bound - given[i], max(1, budget * portions[i] // mass), rest)
            given[i] = given[i] + more
            rest = rest - more
    return np.array(given)


def normal_values(stream_key, dims, deviation, bound, cuts=(), kind=jnp.bfloat16):
    values = deviation * jax.random.normal(stream_key, dims, jnp.float32)
    if cuts:
        values = values * steps_of(stream_key, dims, cuts, -0.22, 0.18)
    return jnp.clip(values, -bound, bound).astype(kind)


def setup_inputs(seed: int = 0) -> dict:
    streams_of = jax.random.split(jax.random.key(seed), 12)
    prompt = normal_values(streams_of[0], (SPAN, D), 1.0, 6.0, ((0, 32), (1, 8)))
    norm_gain = jnp.clip(1.0 + 0.18 * jax.random.normal(streams_of[1], (D,), jnp.float32), 0.1, 1.9)
    kv_weight = normal_values(streams_of[2], (2, D, KV_HEADS * HEAD_DIM), D ** -0.5, 0.0625, ((2, 8),))
    kv_bias = normal_values(streams_of[3], (2, KV_HEADS * HEAD_DIM), 1.0, 6.0, ((1, 8),))
    page_dest_keys = jax.random.split(jax.random.fold_in(streams_of[4], 1), (SPAN // PAGE) // (TOK_DEV // PAGE))
    page_dest_turns = jax.random.permutation(jax.random.fold_in(streams_of[4], 3), (SPAN // PAGE) // (TOK_DEV // PAGE))
    page_dest = jax.vmap(lambda own, number: assign_block(jax.random.fold_in(streams_of[4], 2), own, number, TOK_DEV // PAGE, REPLICAS, 1, MOST, 2))(page_dest_keys, page_dest_turns).reshape((SPAN // PAGE, 1))
    page_row = set_ends(jax.random.randint(streams_of[5], (SPAN // PAGE,), 0, ROWS_DEV), jax.random.fold_in(streams_of[5], 1), 0, ROWS_DEV - 1).astype(jnp.int32)
    page_offset = set_ends(jax.random.randint(streams_of[6], (SPAN // PAGE,), 0, PROMPT - PAGE + 1), jax.random.fold_in(streams_of[6], 1), 0, PROMPT - PAGE).astype(jnp.int32)
    queries = draw_queries(jax.random.fold_in(streams_of[11], 71), 0)
    cache_keys = draw_cache_keys(jax.random.fold_in(streams_of[11], 71), 0)
    cache_values = normal_values(streams_of[9], (ROWS, CONTEXT, KV_HEADS * HEAD_DIM), 1.0, 6.0, ((0, 32), (2, 8)))
    lengths = draw_lengths(jax.random.fold_in(streams_of[11], 71), 0)
    return {"prompt": prompt, "norm_gain": norm_gain, "kv_weight": kv_weight, "kv_bias": kv_bias, "page_dest": page_dest, "page_row": page_row, "page_offset": page_offset, "queries": queries, "cache_keys": cache_keys, "cache_values": cache_values, "lengths": lengths}


def rotate(head_values, positions):
    half_size = head_values.shape[-1] // 2
    freq_index = jnp.arange(half_size, dtype=jnp.float32)
    inverse = jnp.exp(-(2.0 * freq_index / head_values.shape[-1]) * jnp.log(jnp.float32(1000000.0)))
    angles = positions.astype(jnp.float32)[:, None] * inverse[None, :]
    cosine = jnp.cos(angles)[:, None, :]
    sine_part = jnp.sin(angles)[:, None, :]
    first_half = head_values[..., :half_size]
    second_half = head_values[..., half_size:]
    return jnp.concatenate([first_half * cosine - second_half * sine_part, second_half * cosine + first_half * sine_part], -1)

def reference(prompt, norm_gain, kv_weight, kv_bias, page_dest, page_row, page_offset, queries, cache_keys, cache_values, lengths):
    values_float = prompt.astype(jnp.float32)
    inverse_rms = lax.rsqrt(lax.optimization_barrier(jnp.mean(values_float * values_float, -1, keepdims=True)) + 1e-06)
    normed = (values_float * inverse_rms * norm_gain).astype(jnp.bfloat16)
    projected = jnp.einsum('td,sdc->stc', normed.astype(jnp.float32), kv_weight.astype(jnp.float32))
    projected = projected + kv_bias.astype(jnp.float32)[:, None, :]
    token_count = prompt.shape[0]
    page_count = page_offset.shape[0]
    positions = jnp.repeat(page_offset, PAGE) + jnp.tile(jnp.arange(PAGE, dtype=jnp.int32), page_count)
    key_heads = projected[0].reshape(token_count, KV_HEADS, HEAD_DIM)
    new_keys = rotate(key_heads, positions).reshape(token_count, -1).astype(jnp.bfloat16)
    new_values = projected[1].astype(jnp.bfloat16)
    token_dest = jnp.repeat(page_dest[:, 0], PAGE)
    token_row = jnp.repeat(page_row, PAGE)
    groups = Q_HEADS // KV_HEADS
    score_scale = HEAD_DIM ** (-0.5)
    keys_float = new_keys.astype(jnp.float32).reshape(token_count, KV_HEADS, HEAD_DIM)
    values_new = new_values.astype(jnp.float32).reshape(token_count, KV_HEADS, HEAD_DIM)
    row_ids = jnp.arange(ROWS_DEV, dtype=jnp.int32)

    def replica(index):
        start_row = index * ROWS_DEV
        query_block = lax.dynamic_slice_in_dim(queries, start_row, ROWS_DEV, 0).astype(jnp.float32)
        query_block = query_block.reshape(ROWS_DEV, KV_HEADS, groups, HEAD_DIM)
        cache_k = lax.dynamic_slice_in_dim(cache_keys, start_row, ROWS_DEV, 0).astype(jnp.float32)
        cache_k = cache_k.reshape(ROWS_DEV, CONTEXT, KV_HEADS, HEAD_DIM)
        cache_v = lax.dynamic_slice_in_dim(cache_values, start_row, ROWS_DEV, 0).astype(jnp.float32)
        cache_v = cache_v.reshape(ROWS_DEV, CONTEXT, KV_HEADS, HEAD_DIM)
        length_block = lax.dynamic_slice_in_dim(lengths, start_row, ROWS_DEV, 0)
        resident = jnp.einsum('bhgd,bthd->bhgt', query_block, cache_k) * score_scale
        live_mask = jnp.arange(CONTEXT, dtype=jnp.int32)[None, :] < length_block[:, None]
        resident = jnp.where(live_mask[:, None, None, :], resident, -1e+30)
        fresh_scores = jnp.einsum('bhgd,nhd->bhgn', query_block, keys_float) * score_scale
        owned_mask = (token_dest[None, :] == index) & (token_row[None, :] == row_ids[:, None])
        fresh_scores = jnp.where(owned_mask[:, None, None, :], fresh_scores, -1e+30)
        top_score = jnp.maximum(lax.optimization_barrier(jnp.max(resident, -1)), lax.optimization_barrier(jnp.max(fresh_scores, -1)))
        weight_res = jnp.exp(resident - top_score[..., None])
        weight_new = jnp.exp(fresh_scores - top_score[..., None])
        total_weight = lax.optimization_barrier(jnp.sum(weight_res, -1)) + lax.optimization_barrier(jnp.sum(weight_new, -1))
        rounded_res = lax.optimization_barrier(weight_res.astype(jnp.bfloat16)).astype(jnp.float32)
        rounded_new = lax.optimization_barrier(weight_new.astype(jnp.bfloat16)).astype(jnp.float32)
        summed = jnp.einsum('bhgt,bthd->bhgd', rounded_res, cache_v) + jnp.einsum('bhgn,nhd->bhgd', rounded_new, values_new)
        return (summed / total_weight[..., None]).reshape(ROWS_DEV, Q_HEADS * HEAD_DIM).astype(jnp.bfloat16)
    blocks = lax.map(replica, jnp.arange(N_REP, dtype=jnp.int32))
    return blocks.reshape(ROWS_DEV * N_REP, Q_HEADS * HEAD_DIM)
```

```python
import functools

import jax
import jax.numpy as jnp
from jax import lax
from jax.experimental import pallas as pl
from jax.experimental.pallas import tpu as pltpu
from jax.sharding import PartitionSpec as P

D = 8192
HEAD_DIM = 128
PAGE = 8
TOK = 1024
FEAT = 1024
REPLICAS = 32
SLOTS = 8
ROWS = 16
GROUPS = 8
CONTEXT = 512
TILE = 256
STAT = 16
LOW = -1e30
MIB = 1 << 20
NT = (((1,), (1,)), ((), ()))
TN = (((0,), (0,)), ((), ()))
F32 = jnp.float32
BF16 = jnp.bfloat16
VMEM = pl.BlockSpec(memory_space=pltpu.VMEM)
SMEM = pl.BlockSpec(memory_space=pltpu.SMEM)


def cost(flops, bytes_accessed):
    return pl.CostEstimate(flops=flops, bytes_accessed=bytes_accessed, transcendentals=0)


def params(mib):
    return pltpu.CompilerParams(vmem_limit_bytes=mib * MIB)


def device_number(x, y_lo, z, y_hi, core):
    return ((z * 2 + y_hi) * 2 + core) * 8 + x * 2 + y_lo


def permute(array, target):
    pairs = [
        (device_number(x, y, z, h, c), device_number(*target(x, y, z, h, c)))
        for x in range(4)
        for y in range(2)
        for z in range(8)
        for h in range(2)
        for c in range(2)
    ]
    return lax.ppermute(array, ("rep", "tp"), pairs)


def prepare_kernel(own_slot, own, other, gain, first, second, squares_first, squares_second):
    tile = pl.program_id(0)
    ones = jnp.ones((8, FEAT), BF16)

    def scaled(ref):
        values = ref[...].astype(F32)
        return (values * gain[...]).astype(BF16)

    def squares(ref):
        values = ref[...].astype(F32)
        square = values * values
        high = square.astype(BF16)
        low = (square - high.astype(F32)).astype(BF16)
        total = lax.dot_general(ones, high, NT, preferred_element_type=F32)
        total = total + lax.dot_general(ones, low, NT, preferred_element_type=F32)
        total = total[0:1, :]
        top = total.astype(BF16).astype(F32)
        rest = (total - top).astype(BF16).astype(F32)
        return top, rest

    def write(source_a, source_b):
        first[...] = scaled(source_a)
        second[...] = scaled(source_b)
        for source, out in ((source_a, squares_first), (source_b, squares_second)):
            top, rest = squares(source)
            out[pl.ds(tile, 1), :] = top
            out[pl.ds(tile + 4, 1), :] = rest

    @pl.when(tile == 0)
    def _():
        squares_first[...] = jnp.zeros_like(squares_first)
        squares_second[...] = jnp.zeros_like(squares_second)

    @pl.when(own_slot[0] == 0)
    def _():
        write(own, other)

    @pl.when(own_slot[0] != 0)
    def _():
        write(other, own)


def prepare(own_slot, own, other, gain):
    tokens = pl.BlockSpec((TILE, FEAT), lambda i: (i, 0))
    squares = pl.BlockSpec((STAT, TILE), lambda i: (0, 0))
    return pl.pallas_call(
        prepare_kernel,
        grid=(TOK // TILE,),
        in_specs=[SMEM, tokens, tokens, pl.BlockSpec((1, FEAT), lambda i: (0, 0))],
        out_specs=[tokens, tokens, squares, squares],
        out_shape=[
            jax.ShapeDtypeStruct((TOK, FEAT), BF16),
            jax.ShapeDtypeStruct((TOK, FEAT), BF16),
            jax.ShapeDtypeStruct((STAT, TILE), F32),
            jax.ShapeDtypeStruct((STAT, TILE), F32),
        ],
        compiler_params=params(24),
        cost_estimate=cost(16 * TOK * FEAT, 8 * MIB),
        name="prepare",
    )(own_slot, own, other, gain)


def project_kernel(tokens, squares, weight, out):
    tile = pl.program_id(0)
    both = jnp.concatenate([weight[0], weight[1]], axis=1)
    part = lax.dot_general(tokens[...], both, (((1,), (0,)), ((), ())), preferred_element_type=F32)
    out[pl.ds(pl.multiple_of(tile * TILE, TILE), TILE), :] = part.astype(BF16)

    @pl.when(tile == 0)
    def _():
        out[TOK : TOK + STAT, :] = squares[...].astype(BF16)


def project(tokens, squares, weight):
    return pl.pallas_call(
        project_kernel,
        grid=(TOK // TILE,),
        in_specs=[
            pl.BlockSpec((TILE, FEAT), lambda i: (i, 0)),
            pl.BlockSpec((STAT, TILE), lambda i: (0, 0)),
            pl.BlockSpec((2, FEAT, HEAD_DIM), lambda i: (0, 0, 0)),
        ],
        out_specs=pl.BlockSpec((TOK + STAT, 2 * HEAD_DIM), lambda i: (0, 0)),
        out_shape=jax.ShapeDtypeStruct((TOK + STAT, 2 * HEAD_DIM), BF16),
        compiler_params=params(16),
        cost_estimate=cost(2 * TOK * FEAT * 2 * HEAD_DIM, 3 * MIB),
        name="project",
    )(tokens, squares, weight)


def resident_kernel(lengths, queries, keys, values, out, top_out, total_out, sums, tops, totals):
    row = pl.program_id(0)
    scores = lax.dot_general(queries[...], keys[0], NT, preferred_element_type=F32)
    scores = scores * HEAD_DIM**-0.5
    slot = lax.broadcasted_iota(jnp.int32, scores.shape, 1)
    scores = jnp.where(slot < lengths[row], scores, LOW)
    top = jnp.max(scores, axis=1, keepdims=True)
    weights = jnp.exp(scores - top)
    total = jnp.sum(weights, axis=1, keepdims=True)
    place = pl.ds(pl.multiple_of(row * GROUPS, GROUPS), GROUPS)
    sums[place, :] = jnp.dot(weights.astype(BF16), values[0], preferred_element_type=F32)
    tops[place, :] = jnp.broadcast_to(top, (GROUPS, HEAD_DIM))
    totals[place, :] = jnp.broadcast_to(total, (GROUPS, HEAD_DIM))

    @pl.when(row == ROWS - 1)
    def _():
        out[...] = sums[...].T
        top_out[...] = tops[...].T[0:8]
        total_out[...] = totals[...].T[0:8]


def resident(lengths, queries, keys, values):
    cache = pl.BlockSpec((1, CONTEXT, HEAD_DIM), lambda i: (i, 0, 0))
    whole = pl.BlockSpec((HEAD_DIM, HEAD_DIM), lambda i: (0, 0))
    stat = pl.BlockSpec((8, HEAD_DIM), lambda i: (0, 0))
    return pl.pallas_call(
        resident_kernel,
        grid=(ROWS,),
        in_specs=[SMEM, pl.BlockSpec((GROUPS, HEAD_DIM), lambda i: (i, 0)), cache, cache],
        out_specs=[whole, stat, stat],
        out_shape=[
            jax.ShapeDtypeStruct((HEAD_DIM, HEAD_DIM), F32),
            jax.ShapeDtypeStruct((8, HEAD_DIM), F32),
            jax.ShapeDtypeStruct((8, HEAD_DIM), F32),
        ],
        scratch_shapes=[pltpu.VMEM((HEAD_DIM, HEAD_DIM), F32)] * 3,
        compiler_params=params(16),
        cost_estimate=cost(4 * ROWS * GROUPS * CONTEXT * HEAD_DIM, 16 * MIB),
        name="resident",
    )(lengths, queries, keys, values)


def split_stats(top, total):
    top_a = top.astype(BF16).astype(F32)
    top_b = (top - top_a).astype(BF16).astype(F32)
    top_c = (top - top_a) - top_b
    total_a = total.astype(BF16).astype(F32)
    total_b = total - total_a
    rows = [top_a, top_b, top_c, total_a, total_b]
    index = lax.broadcasted_iota(jnp.int32, (STAT, HEAD_DIM), 0)
    tile = jnp.zeros((STAT, HEAD_DIM), F32)
    for number, row in enumerate(rows):
        tile = jnp.where(index == number, row, tile)
    return tile.astype(BF16)


def join_stats(tile):
    stats = tile.astype(F32)
    top = (stats[0:1] + stats[1:2]) + stats[2:3]
    return top, stats[3:4] + stats[4:5]


def finish_kernel(pages, page_rows, core, *refs):
    parts = refs[:8]
    cosine, sine, bias, queries, kept, sent, key_store, value_store = refs[8:]
    squares = jnp.concatenate([part[TOK : TOK + STAT, :] for part in parts], axis=0)
    index = lax.broadcasted_iota(jnp.int32, (8 * STAT, HEAD_DIM), 0)
    for tile in range(TOK // TILE):
        token = slice(tile * TILE, (tile + 1) * TILE)
        chosen = ((index % STAT) < 8) & ((index % 4) == tile)
        total = lax.dot_general(
            squares, jnp.where(chosen, 1.0, 0.0).astype(BF16), TN, preferred_element_type=F32
        )
        inverse = lax.rsqrt(total * (1.0 / D) + 1e-06)
        added = parts[0][token, :].astype(F32)
        for part in parts[1:]:
            added = added + part[token, :].astype(F32)
        keys = added[:, :HEAD_DIM] * inverse + bias[0:1, :]
        values = added[:, HEAD_DIM:] * inverse + bias[1:2, :]
        keys = keys * cosine[token, :] + pltpu.roll(keys, HEAD_DIM // 2, 1) * sine[token, :]
        key_store[token, :] = keys.astype(BF16).astype(F32)
        value_store[token, :] = values.astype(BF16).astype(F32)

    lane_row = lax.broadcasted_iota(jnp.int32, (PAGE, HEAD_DIM), 1) // GROUPS

    def attend(replica):
        key_pages, value_pages, masks = [], [], []
        for slot in range(SLOTS):
            page = pages[replica * SLOTS + slot]
            place = pl.ds(pl.multiple_of(page * PAGE, PAGE), PAGE)
            key_pages.append(key_store[place, :])
            value_pages.append(value_store[place, :])
            masks.append(lane_row == page_rows[replica * SLOTS + slot])
        keys = jnp.concatenate(key_pages, axis=0).astype(BF16)
        values = jnp.concatenate(value_pages, axis=0).astype(BF16)
        scores = lax.dot_general(keys, queries[replica], NT, preferred_element_type=F32)
        scores = scores * HEAD_DIM**-0.5
        scores = jnp.where(jnp.concatenate(masks, axis=0), scores, LOW)
        top = jnp.max(scores, axis=0, keepdims=True)
        weights = jnp.exp(scores - top)
        total = jnp.sum(weights, axis=0, keepdims=True)
        summed = lax.dot_general(values, weights.astype(BF16), TN, preferred_element_type=F32)
        return summed.astype(BF16), split_stats(top, total)

    for flip, out in ((1, sent), (0, kept)):

        def block(step, carry, flip=flip, out=out):
            for inner in range(4):
                place = step * 4 + inner
                replica = place * 2 + (core[0] + flip) % 2
                summed, stats = attend(replica)
                out[place, 0:HEAD_DIM, :] = summed
                out[place, HEAD_DIM : HEAD_DIM + STAT, :] = stats
            return carry

        lax.fori_loop(0, 4, block, 0)


def finish(pages, page_rows, core, parts, cosine, sine, bias, queries):
    partial = jax.ShapeDtypeStruct((16, HEAD_DIM + STAT, HEAD_DIM), BF16)
    return pl.pallas_call(
        finish_kernel,
        in_specs=[SMEM] * 3 + [VMEM] * 12,
        out_specs=[VMEM, VMEM],
        out_shape=[partial, partial],
        scratch_shapes=[pltpu.VMEM((TOK, HEAD_DIM), F32)] * 2,
        compiler_params=params(32),
        cost_estimate=cost(4 * 2048 * 128 * 128, 16 * MIB),
        name="finish",
    )(pages, page_rows, core, *parts, cosine, sine, bias, queries)


def merge_kernel(left, right, out):
    def block(step, carry):
        for inner in range(4):
            place = step * 4 + inner
            left_top, left_total = join_stats(left[place, HEAD_DIM:, :])
            right_top, right_total = join_stats(right[place, HEAD_DIM:, :])
            top = jnp.maximum(left_top, right_top)
            left_scale = jnp.exp(left_top - top)
            right_scale = jnp.exp(right_top - top)
            summed = left[place, 0:HEAD_DIM, :].astype(F32) * left_scale
            summed = summed + right[place, 0:HEAD_DIM, :].astype(F32) * right_scale
            out[place, 0:HEAD_DIM, :] = summed.astype(BF16)
            total = left_total * left_scale + right_total * right_scale
            out[place, HEAD_DIM:, :] = split_stats(top, total)
        return carry

    lax.fori_loop(0, 4, block, 0)


def merge(left, right):
    return pl.pallas_call(
        merge_kernel,
        in_specs=[VMEM, VMEM],
        out_specs=VMEM,
        out_shape=jax.ShapeDtypeStruct((16, HEAD_DIM + STAT, HEAD_DIM), BF16),
        compiler_params=params(16),
        cost_estimate=cost(16 * 128 * 128 * 4, 2 * MIB),
        name="merge",
    )(left, right)


def conclude_kernel(received, sums, tops, totals, out, store):
    stats = [join_stats(received[i, HEAD_DIM:, :]) for i in range(16)]
    top = tops[0:1]
    for part_top, _ in stats:
        top = jnp.maximum(top, part_top)
    scale = jnp.exp(tops[0:1] - top)
    summed = sums[...] * scale
    total = totals[0:1] * scale
    for i, (part_top, part_total) in enumerate(stats):
        scale = jnp.exp(part_top - top)
        summed = summed + received[i, 0:HEAD_DIM, :].astype(F32) * scale
        total = total + part_total * scale
    store[...] = (summed / total).T
    for group in range(GROUPS):
        columns = slice(group * HEAD_DIM, (group + 1) * HEAD_DIM)
        out[:, columns] = store[pl.ds(group, ROWS, stride=GROUPS), :].astype(BF16)


def conclude(received, sums, tops, totals):
    return pl.pallas_call(
        conclude_kernel,
        in_specs=[VMEM] * 4,
        out_specs=VMEM,
        out_shape=jax.ShapeDtypeStruct((ROWS, GROUPS * HEAD_DIM), BF16),
        scratch_shapes=[pltpu.VMEM((HEAD_DIM, HEAD_DIM), F32)],
        compiler_params=params(16),
        cost_estimate=cost(16 * 128 * 128 * 4, MIB),
        name="conclude",
    )(received, sums, tops, totals)


def angle_tables(page_offset):
    half = HEAD_DIM // 2
    index = jnp.arange(half, dtype=F32)
    inverse = jnp.exp(-(2.0 * index / HEAD_DIM) * jnp.log(F32(1000000.0)))
    positions = jnp.repeat(page_offset, PAGE) + jnp.tile(
        jnp.arange(PAGE, dtype=jnp.int32), page_offset.shape[0]
    )
    angles = positions.astype(F32)[:, None] * inverse[None, :]
    cosine, sine = jnp.cos(angles), jnp.sin(angles)
    return jnp.concatenate([cosine, cosine], 1), jnp.concatenate([-sine, sine], 1)


def page_tables(page_dest, page_row):
    dest = page_dest[:, 0]
    count = dest.shape[0]
    number = jnp.arange(count, dtype=jnp.int32)
    earlier = (dest[None, :] == dest[:, None]) & (number[None, :] < number[:, None])
    slot = dest * SLOTS + jnp.sum(earlier.astype(jnp.int32), 1)
    match = slot[None, :] == jnp.arange(REPLICAS * SLOTS, dtype=jnp.int32)[:, None]
    pages = jnp.max(jnp.where(match, number[None, :], 0), 1)
    rows = jnp.max(jnp.where(match, page_row[None, :], -1), 1)
    return pages, rows


def per_device(
    prompt,
    norm_gain,
    kv_weight,
    kv_bias,
    page_dest,
    page_row,
    page_offset,
    queries,
    cache_keys,
    cache_values,
    lengths,
):
    tp = lax.axis_index("tp")
    core = lax.axis_index("rep") % 2
    x, y = tp // 2, tp % 2
    query_heads = queries.reshape(ROWS * GROUPS, HEAD_DIM)
    all_queries = lax.all_gather(query_heads, "rep", axis=0, tiled=False)
    other = permute(prompt, lambda x, y, z, h, c: (x, y, z, h, 1 - c))

    order = (2, 1, 3, 0)
    weights = {}
    for dx in order:
        block = ((x + dx) % 4) * 2 + (y + core) % 2
        rows = lax.dynamic_slice(kv_weight, (0, block * FEAT, 0), (2, FEAT, HEAD_DIM))
        weights[dx] = permute(rows, lambda x, y, z, h, c, dx=dx: ((x + dx) % 4, y ^ c, z, h, y))

    gain = lax.dynamic_slice(norm_gain, (tp * FEAT,), (FEAT,)).reshape(1, FEAT)
    own_slot = ((y + core) % 2).reshape(1)
    first, second, squares_first, squares_second = prepare(own_slot, prompt, other, gain)
    tokens, squares = (first, second), (squares_first, squares_second)

    sums, tops, totals = resident(lengths, query_heads, cache_keys, cache_values)
    cosine, sine = angle_tables(page_offset)
    pages, page_rows = page_tables(page_dest, page_row)

    parts = []
    for dx in order:
        for k in range(2):
            part = project(tokens[k], squares[k], weights[dx])
            parts.append(
                permute(part, lambda x, y, z, h, c, dx=dx, k=k: ((x - dx) % 4, c, z, h, y ^ k))
            )

    kept, sent = finish(
        pages, page_rows, core.reshape(1), parts, cosine, sine, kv_bias.astype(F32), all_queries
    )
    arrived = permute(sent, lambda x, y, z, h, c: (x, y, z, h, 1 - c))
    merged = merge(kept, arrived)
    groups = [[zy * 2 + c for zy in range(16)] for c in range(2)]
    received = lax.all_to_all(merged, "rep", 0, 0, tiled=True, axis_index_groups=groups)
    return conclude(received, sums, tops, totals)


def solution(mesh):
    placed = (
        P("rep", "tp"),
        P(),
        P(None, None, "tp"),
        P(None, "tp"),
        P("rep", None),
        P("rep"),
        P("rep"),
        P("rep", "tp"),
        P("rep", None, "tp"),
        P("rep", None, "tp"),
        P("rep"),
    )
    return jax.shard_map(
        per_device, mesh=mesh, in_specs=placed, out_specs=P("rep", "tp"), check_vma=False
    )
```

```python
import functools

import jax
import jax.numpy as jnp
from jax import lax
from jax.experimental import pallas as pl
from jax.experimental.pallas import tpu as pltpu
from jax.sharding import PartitionSpec as P

D = 8192
HEAD_DIM = 128
PAGE = 8
TOK = 1024
FEAT = 1024
REPLICAS = 32
SLOTS = 8
ROWS = 16
GROUPS = 8
CONTEXT = 512
TILE = 128
CHUNKS = (640, 384)
STEP = 32
STAT = 16
LOW = -1e30
MIB = 1 << 20
NT = (((1,), (1,)), ((), ()))
TN = (((0,), (0,)), ((), ()))
F32 = jnp.float32
BF16 = jnp.bfloat16
VMEM = pl.BlockSpec(memory_space=pltpu.VMEM)
SMEM = pl.BlockSpec(memory_space=pltpu.SMEM)
HBM = pl.BlockSpec(memory_space=pltpu.HBM)


def cost(flops, bytes_accessed):
    return pl.CostEstimate(flops=flops, bytes_accessed=bytes_accessed, transcendentals=0)


def params(mib):
    return pltpu.CompilerParams(vmem_limit_bytes=mib * MIB)


def device_number(x, y_lo, z, y_hi, core):
    return ((z * 2 + y_hi) * 2 + core) * 8 + x * 2 + y_lo


def permute(array, target):
    pairs = [
        (device_number(x, y, z, h, c), device_number(*target(x, y, z, h, c)))
        for x in range(4)
        for y in range(2)
        for z in range(8)
        for h in range(2)
        for c in range(2)
    ]
    return lax.ppermute(array, ("rep", "tp"), pairs)


def after(value, other):
    if other is None:
        return value
    return lax.optimization_barrier((value, other))[0]


def project_kernel(start, same, own, other, own_gain, other_gain, *refs):
    weights, outs = refs[0:8], refs[8:12]
    tokens_store, scaled, folded, store, results, arrived, left = refs[12:]
    count = other.shape[0]
    copies = [
        pltpu.make_async_copy(own.at[pl.ds(start, count), :], tokens_store.at[0], arrived.at[8]),
        pltpu.make_async_copy(other, tokens_store.at[1], arrived.at[9]),
    ]
    for head in (2, 1, 3, 0):
        for i in (head, head + 4):
            copies.append(pltpu.make_async_copy(weights[i], store.at[i], arrived.at[i]))
    for copy in copies[:4]:
        copy.start()
    ones = jnp.ones((8, TILE), BF16)

    copies[0].wait()
    copies[1].wait()
    for copy in copies[4:]:
        copy.start()

    def scale(step, carry):
        rows = pl.ds(pl.multiple_of(step * STEP, STEP), STEP)
        own_values, other_values = (tokens_store[i, rows, :].astype(F32) for i in (0, 1))
        square = own_values * own_values + other_values * other_values
        sums = square[:, 0:TILE]
        for part in range(1, FEAT // TILE):
            sums = sums + square[:, part * TILE : (part + 1) * TILE]
        folded[rows, :] = sums
        scaled[1 - same[0], rows, :] = (own_values * own_gain[...]).astype(BF16)
        scaled[same[0], rows, :] = (other_values * other_gain[...]).astype(BF16)
        return carry

    lax.fori_loop(0, count // STEP, scale, 0)
    high = folded[...].astype(BF16)
    low = (folded[...] - high.astype(F32)).astype(BF16)
    total = lax.dot_general(ones, high, NT, preferred_element_type=F32)
    total = (total + lax.dot_general(ones, low, NT, preferred_element_type=F32))[0:1, :]
    top = total.astype(BF16).astype(F32)
    rest = total - top
    index = lax.broadcasted_iota(jnp.int32, (STAT, TILE), 0)
    table = jnp.zeros((STAT, TILE), F32)
    for tile in range(count // TILE):
        token = slice(tile * TILE, (tile + 1) * TILE)
        table = jnp.where(index == tile, top[:, token], table)
        table = jnp.where(index == tile + 8, rest[:, token], table)
    table = jnp.concatenate([table, jnp.zeros_like(table)], axis=1).astype(BF16)

    leaving = []
    for number, head in enumerate((2, 1, 3, 0)):
        copies[2 + 2 * number].wait()
        copies[3 + 2 * number].wait()
        near = jnp.concatenate([store[head, 0], store[head, 1]], axis=1)
        far = jnp.concatenate([store[head + 4, 0], store[head + 4, 1]], axis=1)
        for tile in range(0, count, TILE):
            rows = slice(tile, tile + TILE)
            part = jnp.dot(scaled[0, rows, :], near, preferred_element_type=F32)
            part = part + jnp.dot(scaled[1, rows, :], far, preferred_element_type=F32)
            results[head, rows, :] = part.astype(BF16)
        results[head, count:, :] = table
        leaving.append(pltpu.make_async_copy(results.at[head], outs[head], left.at[head]))
        leaving[-1].start()
    for copy in leaving:
        copy.wait()


def project(same, prompt, start, other, own_gain, other_gain, near, far):
    count = other.shape[0]
    return pl.pallas_call(
        functools.partial(project_kernel, start),
        in_specs=[SMEM, HBM, HBM, VMEM, VMEM] + [HBM] * 8,
        out_specs=[HBM] * 4,
        out_shape=[jax.ShapeDtypeStruct((count + STAT, 2 * HEAD_DIM), BF16)] * 4,
        scratch_shapes=[
            pltpu.VMEM((2, count, FEAT), BF16),
            pltpu.VMEM((2, count, FEAT), BF16),
            pltpu.VMEM((count, TILE), F32),
            pltpu.VMEM((8, 2, FEAT, HEAD_DIM), BF16),
            pltpu.VMEM((4, count + STAT, 2 * HEAD_DIM), BF16),
            pltpu.SemaphoreType.DMA((10,)),
            pltpu.SemaphoreType.DMA((4,)),
        ],
        compiler_params=params(40),
        cost_estimate=cost(2 * count * 2 * FEAT * 8 * HEAD_DIM, 6 * MIB),
        name="project",
    )(same, prompt, other, own_gain, other_gain, *near, *far)


def resident_kernel(lengths, queries, keys, values, out, top_out, total_out, sums, tops, totals):
    row = pl.program_id(0)
    scores = lax.dot_general(queries[...], keys[0], NT, preferred_element_type=F32)
    scores = scores * HEAD_DIM**-0.5
    slot = lax.broadcasted_iota(jnp.int32, scores.shape, 1)
    scores = jnp.where(slot < lengths[row], scores, LOW)
    top = jnp.max(scores, axis=1, keepdims=True)
    weights = jnp.exp(scores - top)
    total = jnp.sum(weights, axis=1, keepdims=True)
    place = pl.ds(pl.multiple_of(row * GROUPS, GROUPS), GROUPS)
    sums[place, :] = jnp.dot(weights.astype(BF16), values[0], preferred_element_type=F32)
    tops[place, :] = jnp.broadcast_to(top, (GROUPS, HEAD_DIM))
    totals[place, :] = jnp.broadcast_to(total, (GROUPS, HEAD_DIM))

    @pl.when(row == ROWS - 1)
    def _():
        out[...] = sums[...].T
        top_out[...] = tops[...].T[0:8]
        total_out[...] = totals[...].T[0:8]


def resident(lengths, queries, keys, values):
    cache = pl.BlockSpec((1, CONTEXT, HEAD_DIM), lambda i: (i, 0, 0))
    whole = pl.BlockSpec((HEAD_DIM, HEAD_DIM), lambda i: (0, 0))
    stat = pl.BlockSpec((8, HEAD_DIM), lambda i: (0, 0))
    return pl.pallas_call(
        resident_kernel,
        grid=(ROWS,),
        in_specs=[SMEM, pl.BlockSpec((GROUPS, HEAD_DIM), lambda i: (i, 0)), cache, cache],
        out_specs=[whole, stat, stat],
        out_shape=[
            jax.ShapeDtypeStruct((HEAD_DIM, HEAD_DIM), F32),
            jax.ShapeDtypeStruct((8, HEAD_DIM), F32),
            jax.ShapeDtypeStruct((8, HEAD_DIM), F32),
        ],
        scratch_shapes=[pltpu.VMEM((HEAD_DIM, HEAD_DIM), F32)] * 3,
        compiler_params=params(16),
        cost_estimate=cost(4 * ROWS * GROUPS * CONTEXT * HEAD_DIM, 16 * MIB),
        name="resident",
    )(lengths, queries, keys, values)


def split_stats(top, total):
    top_a = top.astype(BF16).astype(F32)
    top_b = (top - top_a).astype(BF16).astype(F32)
    top_c = (top - top_a) - top_b
    total_a = total.astype(BF16).astype(F32)
    total_b = total - total_a
    rows = [top_a, top_b, top_c, total_a, total_b]
    index = lax.broadcasted_iota(jnp.int32, (STAT, HEAD_DIM), 0)
    tile = jnp.zeros((STAT, HEAD_DIM), F32)
    for number, row in enumerate(rows):
        tile = jnp.where(index == number, row, tile)
    return tile.astype(BF16)


def join_stats(tile):
    stats = tile.astype(F32)
    top = (stats[0:1] + stats[1:2]) + stats[2:3]
    return top, stats[3:4] + stats[4:5]


def finish_chunk(parts, cosine, sine, bias, start, key_out, value_out, place):
    count = parts[0].shape[0] - STAT
    squares = jnp.concatenate([part[count:, 0:TILE] for part in parts], axis=0)
    index = lax.broadcasted_iota(jnp.int32, (len(parts) * STAT, HEAD_DIM), 0)
    for tile in range(count // TILE):
        token = slice(tile * TILE, (tile + 1) * TILE)
        table = slice(start + tile * TILE, start + (tile + 1) * TILE)
        target = slice(place + tile * TILE, place + (tile + 1) * TILE)
        chosen = (index % 8) == tile
        total = lax.dot_general(
            squares, jnp.where(chosen, 1.0, 0.0).astype(BF16), TN, preferred_element_type=F32
        )
        inverse = lax.rsqrt(total * (1.0 / D) + 1e-06)
        added = parts[0][token, :].astype(F32)
        for part in parts[1:]:
            added = added + part[token, :].astype(F32)
        keys = added[:, :HEAD_DIM] * inverse + bias[0:1, :]
        values = added[:, HEAD_DIM:] * inverse + bias[1:2, :]
        keys = keys * cosine[table, :] + pltpu.roll(keys, HEAD_DIM // 2, 1) * sine[table, :]
        key_out[target, :] = keys.astype(BF16).astype(F32)
        value_out[target, :] = values.astype(BF16).astype(F32)


def finish_kernel(start, *refs):
    finish_chunk(refs[:4], refs[4], refs[5], refs[6], start, refs[7], refs[8], 0)


def finish(parts, cosine, sine, bias, start):
    count = parts[0].shape[0] - STAT
    return pl.pallas_call(
        functools.partial(finish_kernel, start),
        in_specs=[VMEM] * 7,
        out_specs=[VMEM] * 2,
        out_shape=[jax.ShapeDtypeStruct((count, HEAD_DIM), F32)] * 2,
        compiler_params=params(24),
        cost_estimate=cost(20 * count * 256, 2 * MIB),
        name="finish",
    )(*parts, cosine, sine, bias)


def attend_kernel(starts, pages, page_rows, place_of, *refs):
    parts, (cosine, sine, bias, near_queries, far_queries) = refs[:4], refs[4:9]
    done = refs[9 : 9 + 2 * (len(starts) - 1)]
    kept, sent, key_store, value_store = refs[9 + len(done) :]
    for number, start in enumerate(starts[:-1]):
        count = done[2 * number].shape[0]
        key_store[start : start + count, :] = done[2 * number][...]
        value_store[start : start + count, :] = done[2 * number + 1][...]
    finish_chunk(parts, cosine, sine, bias, starts[-1], key_store, value_store, starts[-1])

    core = place_of[0]
    lane_row = lax.broadcasted_iota(jnp.int32, (PAGE, HEAD_DIM), 1) // GROUPS

    def attend(replica, query):
        key_pages, value_pages, masks = [], [], []
        for slot in range(SLOTS):
            page = pages[replica * SLOTS + slot]
            place = pl.ds(pl.multiple_of(page * PAGE, PAGE), PAGE)
            key_pages.append(key_store[place, :])
            value_pages.append(value_store[place, :])
            masks.append(lane_row == page_rows[replica * SLOTS + slot])
        keys = jnp.concatenate(key_pages, axis=0).astype(BF16)
        values = jnp.concatenate(value_pages, axis=0).astype(BF16)
        scores = lax.dot_general(keys, query, NT, preferred_element_type=F32)
        scores = scores * HEAD_DIM**-0.5
        scores = jnp.where(jnp.concatenate(masks, axis=0), scores, LOW)
        top = jnp.max(scores, axis=0, keepdims=True)
        weights = jnp.exp(scores - top)
        total = jnp.sum(weights, axis=0, keepdims=True)
        summed = lax.dot_general(values, weights.astype(BF16), TN, preferred_element_type=F32)
        return summed.astype(BF16), split_stats(top, total)

    for flip, queries, out in ((1, far_queries, sent), (0, near_queries, kept)):

        def block(step, carry, flip=flip, queries=queries, out=out):
            for inner in range(4):
                place = step * 4 + inner
                replica = place * 2 + (core + flip) % 2
                summed, stats = attend(replica, queries[place])
                out[place, 0:HEAD_DIM, :] = summed
                out[place, HEAD_DIM : HEAD_DIM + STAT, :] = stats
            return carry

        lax.fori_loop(0, 4, block, 0)


def attend(starts, pages, page_rows, place_of, parts, cosine, sine, bias, near, far, done):
    partial = jax.ShapeDtypeStruct((16, HEAD_DIM + STAT, HEAD_DIM), BF16)
    return pl.pallas_call(
        functools.partial(attend_kernel, starts),
        in_specs=[SMEM] * 3 + [VMEM] * (9 + len(done)),
        out_specs=[VMEM, VMEM],
        out_shape=[partial, partial],
        scratch_shapes=[pltpu.VMEM((TOK, HEAD_DIM), F32)] * 2,
        compiler_params=params(32),
        cost_estimate=cost(4 * 2048 * 128 * 128, 16 * MIB),
        name="attend",
    )(pages, page_rows, place_of, *parts, cosine, sine, bias, near, far, *done)


def merge_kernel(left, right, out):
    def block(step, carry):
        for inner in range(4):
            place = step * 4 + inner
            left_top, left_total = join_stats(left[place, HEAD_DIM:, :])
            right_top, right_total = join_stats(right[place, HEAD_DIM:, :])
            top = jnp.maximum(left_top, right_top)
            left_scale = jnp.exp(left_top - top)
            right_scale = jnp.exp(right_top - top)
            summed = left[place, 0:HEAD_DIM, :].astype(F32) * left_scale
            summed = summed + right[place, 0:HEAD_DIM, :].astype(F32) * right_scale
            out[place, 0:HEAD_DIM, :] = summed.astype(BF16)
            total = left_total * left_scale + right_total * right_scale
            out[place, HEAD_DIM:, :] = split_stats(top, total)
        return carry

    lax.fori_loop(0, 4, block, 0)


def merge(left, right):
    return pl.pallas_call(
        merge_kernel,
        in_specs=[VMEM, VMEM],
        out_specs=VMEM,
        out_shape=jax.ShapeDtypeStruct((16, HEAD_DIM + STAT, HEAD_DIM), BF16),
        compiler_params=params(16),
        cost_estimate=cost(16 * 128 * 128 * 4, 2 * MIB),
        name="merge",
    )(left, right)


def conclude_kernel(received, sums, tops, totals, out, store):
    stats = [join_stats(received[i, HEAD_DIM:, :]) for i in range(16)]
    top = tops[0:1]
    for part_top, _ in stats:
        top = jnp.maximum(top, part_top)
    scale = jnp.exp(tops[0:1] - top)
    summed = sums[...] * scale
    total = totals[0:1] * scale
    for i, (part_top, part_total) in enumerate(stats):
        scale = jnp.exp(part_top - top)
        summed = summed + received[i, 0:HEAD_DIM, :].astype(F32) * scale
        total = total + part_total * scale
    store[...] = (summed / total).T
    for group in range(GROUPS):
        columns = slice(group * HEAD_DIM, (group + 1) * HEAD_DIM)
        out[:, columns] = store[pl.ds(group, ROWS, stride=GROUPS), :].astype(BF16)


def conclude(received, sums, tops, totals):
    return pl.pallas_call(
        conclude_kernel,
        in_specs=[VMEM] * 4,
        out_specs=VMEM,
        out_shape=jax.ShapeDtypeStruct((ROWS, GROUPS * HEAD_DIM), BF16),
        scratch_shapes=[pltpu.VMEM((HEAD_DIM, HEAD_DIM), F32)],
        compiler_params=params(16),
        cost_estimate=cost(16 * 128 * 128 * 4, MIB),
        name="conclude",
    )(received, sums, tops, totals)


def angle_tables(page_offset):
    half = HEAD_DIM // 2
    index = jnp.arange(half, dtype=F32)
    inverse = jnp.exp(-(2.0 * index / HEAD_DIM) * jnp.log(F32(1000000.0)))
    positions = jnp.repeat(page_offset, PAGE) + jnp.tile(
        jnp.arange(PAGE, dtype=jnp.int32), page_offset.shape[0]
    )
    angles = positions.astype(F32)[:, None] * inverse[None, :]
    cosine, sine = jnp.cos(angles), jnp.sin(angles)
    return jnp.concatenate([cosine, cosine], 1), jnp.concatenate([-sine, sine], 1)


def page_tables(page_dest, page_row):
    dest = page_dest[:, 0]
    count = dest.shape[0]
    number = jnp.arange(count, dtype=jnp.int32)
    earlier = (dest[None, :] == dest[:, None]) & (number[None, :] < number[:, None])
    slot = dest * SLOTS + jnp.sum(earlier.astype(jnp.int32), 1)
    match = slot[None, :] == jnp.arange(REPLICAS * SLOTS, dtype=jnp.int32)[:, None]
    pages = jnp.max(jnp.where(match, number[None, :], 0), 1)
    rows = jnp.max(jnp.where(match, page_row[None, :], -1), 1)
    return pages, rows


def per_device(
    prompt,
    norm_gain,
    kv_weight,
    kv_bias,
    page_dest,
    page_row,
    page_offset,
    queries,
    cache_keys,
    cache_values,
    lengths,
):
    tp, rep = lax.axis_index("tp"), lax.axis_index("rep")
    core = rep % 2
    x, y = tp // 2, tp % 2
    starts = [sum(CHUNKS[:i]) for i in range(len(CHUNKS))]

    def rows_of(number, follows=None):
        start, count = starts[number], CHUNKS[number]
        return after(prompt, follows)[start : start + count]

    def swap(rows):
        return permute(rows, lambda x, y, z, h, c: (x, 1 - y, z, h, c))

    def weight_rows(block, follows=None):
        return lax.dynamic_slice(
            after(kv_weight, follows), (0, block * FEAT, 0), (2, FEAT, HEAD_DIM)
        )

    def fetch(dx, rows):
        near = permute(rows, lambda x, y, z, h, c: ((x + dx) % 4, y, z, h, c))
        return near, permute(near, lambda x, y, z, h, c: (x, y, z, h, 1 - c))

    def wanted(dx, follows):
        return weight_rows(((x + dx) % 4) * 2 + core, follows)

    first_rows = rows_of(0)
    others = [swap(first_rows)]
    one = wanted(1, first_rows)
    three = wanted(3, first_rows)
    two = wanted(2, (one, three))
    near, far = [None] * 4, [None] * 4
    near[1], far[1] = fetch(1, one)
    near[3], far[3] = fetch(3, three)
    near[2], far[2] = fetch(2, two)
    query_heads = after(queries, two).reshape(ROWS * GROUPS, HEAD_DIM)
    groups = [[zy * 2 + c for zy in range(16)] for c in range(2)]
    near_queries = lax.all_to_all(
        jnp.broadcast_to(query_heads, (16, ROWS * GROUPS, HEAD_DIM)),
        "rep", 0, 0, tiled=True, axis_index_groups=groups,
    )
    cosine, sine = angle_tables(page_offset)
    others.append(swap(rows_of(1, (near[1], cosine, sine))))
    near[0] = weight_rows(x * 2 + core, (far[1], far[3]))
    far[0] = weight_rows(x * 2 + 1 - core, (far[1], far[3]))
    far_queries = permute(
        after(near_queries, near[2]), lambda x, y, z, h, c: (x, y, z, h, 1 - c)
    )

    def gain(block):
        return lax.dynamic_slice(norm_gain, (block * FEAT,), (FEAT,)).reshape(1, FEAT)

    own_gain, other_gain = gain(tp), gain(x * 2 + 1 - y)
    same = (y == core).astype(jnp.int32).reshape(1)
    bias = kv_bias.astype(F32)

    sums, tops, totals = resident(lengths, query_heads, cache_keys, cache_values)
    pages, page_rows = page_tables(page_dest, page_row)

    done = []
    for start, other in zip(starts, others):
        outs = project(same, prompt, start, other, own_gain, other_gain, near, far)
        parts = [outs[0]] + [
            permute(outs[dx], lambda x, y, z, h, c, dx=dx: ((x - dx) % 4, y, z, h, c))
            for dx in (1, 2, 3)
        ]
        if start != starts[-1]:
            done.extend(finish(parts, cosine, sine, bias, start))

    place_of = core.reshape(1)
    kept, sent = attend(
        starts, pages, page_rows, place_of, parts, cosine, sine, bias, near_queries, far_queries, done
    )
    arrived = permute(sent, lambda x, y, z, h, c: (x, y, z, h, 1 - c))
    merged = merge(kept, arrived)
    received = lax.all_to_all(merged, "rep", 0, 0, tiled=True, axis_index_groups=groups)
    return conclude(received, sums, tops, totals)


def solution(mesh):
    placed = (
        P("rep", "tp"),
        P(),
        P(None, None, "tp"),
        P(None, "tp"),
        P("rep", None),
        P("rep"),
        P("rep"),
        P("rep", "tp"),
        P("rep", None, "tp"),
        P("rep", None, "tp"),
        P("rep"),
    )
    return jax.shard_map(
        per_device, mesh=mesh, in_specs=placed, out_specs=P("rep", "tp"), check_vma=False
    )
```

```python
import functools

import jax
import jax.numpy as jnp
from jax import lax
from jax.experimental import pallas as pl
from jax.experimental.pallas import tpu as pltpu
from jax.sharding import PartitionSpec as P

D = 8192
HEAD_DIM = 128
PAGE = 8
TOK = 1024
FEAT = 1024
REPLICAS = 32
SLOTS = 8
ROWS = 16
GROUPS = 8
CONTEXT = 512
TILE = 128
CHUNKS = (512, 512)
STEP = 32
STAT = 16
LOW = -1e30
MIB = 1 << 20
NT = (((1,), (1,)), ((), ()))
TN = (((0,), (0,)), ((), ()))
F32 = jnp.float32
BF16 = jnp.bfloat16
VMEM = pl.BlockSpec(memory_space=pltpu.VMEM)
SMEM = pl.BlockSpec(memory_space=pltpu.SMEM)
HBM = pl.BlockSpec(memory_space=pltpu.HBM)


def cost(flops, bytes_accessed):
    return pl.CostEstimate(flops=flops, bytes_accessed=bytes_accessed, transcendentals=0)


def params(mib):
    return pltpu.CompilerParams(vmem_limit_bytes=mib * MIB)


def device_number(x, y_lo, z, y_hi, core):
    return ((z * 2 + y_hi) * 2 + core) * 8 + x * 2 + y_lo


def permute(array, target):
    pairs = [
        (device_number(x, y, z, h, c), device_number(*target(x, y, z, h, c)))
        for x in range(4)
        for y in range(2)
        for z in range(8)
        for h in range(2)
        for c in range(2)
    ]
    return lax.ppermute(array, ("rep", "tp"), pairs)


def after(value, other):
    if other is None:
        return value
    return lax.optimization_barrier((value, other))[0]


def project_kernel(start, same, own, other, *refs):
    weights, outs = refs[0:8], refs[8:12]
    tokens, folded, store, results, arrived, left = refs[12:]
    count = other.shape[0]
    own_place = 1 - same[0]
    copies = [
        pltpu.make_async_copy(own.at[pl.ds(start, count), :], tokens.at[own_place], arrived.at[8]),
        pltpu.make_async_copy(other, tokens.at[1 - own_place], arrived.at[9]),
    ]
    heads = (2, 1, 3, 0)
    for head in heads:
        for i in (head, head + 4):
            copies.append(pltpu.make_async_copy(weights[i], store.at[i], arrived.at[i]))
    for copy in copies:
        copy.start()
    copies[0].wait()
    copies[1].wait()

    def square(step, carry):
        rows = pl.ds(pl.multiple_of(step * STEP, STEP), STEP)
        left_values, right_values = (tokens[i, rows, :].astype(F32) for i in (0, 1))
        squares = left_values * left_values + right_values * right_values
        sums = squares[:, 0:TILE]
        for part in range(1, FEAT // TILE):
            sums = sums + squares[:, part * TILE : (part + 1) * TILE]
        folded[rows, :] = sums
        return carry

    lax.fori_loop(0, count // STEP, square, 0)
    ones = jnp.ones((8, TILE), BF16)
    high = folded[...].astype(BF16)
    low = (folded[...] - high.astype(F32)).astype(BF16)
    total = lax.dot_general(ones, high, NT, preferred_element_type=F32)
    total = (total + lax.dot_general(ones, low, NT, preferred_element_type=F32))[0:1, :]
    top = total.astype(BF16).astype(F32)
    rest = total - top

    index = lax.broadcasted_iota(jnp.int32, (STAT, TILE), 0)
    table = jnp.zeros((STAT, TILE), F32)
    for tile in range(count // TILE):
        token = slice(tile * TILE, (tile + 1) * TILE)
        table = jnp.where(index == tile, top[:, token], table)
        table = jnp.where(index == tile + 8, rest[:, token], table)
    table = jnp.concatenate([table, jnp.zeros_like(table)], axis=1).astype(BF16)

    leaving = []
    for number, head in enumerate(heads):
        copies[2 + 2 * number].wait()
        copies[3 + 2 * number].wait()
        near = jnp.concatenate([store[head, 0], store[head, 1]], axis=1)
        far = jnp.concatenate([store[head + 4, 0], store[head + 4, 1]], axis=1)
        for tile in range(0, count, TILE):
            rows = slice(tile, tile + TILE)
            part = jnp.dot(tokens[0, rows, :], near, preferred_element_type=F32)
            part = part + jnp.dot(tokens[1, rows, :], far, preferred_element_type=F32)
            results[head, rows, :] = part.astype(BF16)
        results[head, count:, :] = table
        leaving.append(pltpu.make_async_copy(results.at[head], outs[head], left.at[head]))
        leaving[-1].start()
    for copy in leaving:
        copy.wait()


def project(same, prompt, start, other, near, far):
    count = other.shape[0]
    return pl.pallas_call(
        functools.partial(project_kernel, start),
        in_specs=[SMEM] + [HBM] * 10,
        out_specs=[HBM] * 4,
        out_shape=[jax.ShapeDtypeStruct((count + STAT, 2 * HEAD_DIM), BF16)] * 4,
        scratch_shapes=[
            pltpu.VMEM((2, count, FEAT), BF16),
            pltpu.VMEM((count, TILE), F32),
            pltpu.VMEM((8, 2, FEAT, HEAD_DIM), BF16),
            pltpu.VMEM((4, count + STAT, 2 * HEAD_DIM), BF16),
            pltpu.SemaphoreType.DMA((10,)),
            pltpu.SemaphoreType.DMA((4,)),
        ],
        compiler_params=params(14),
        cost_estimate=cost(1, 1),
        name="project",
    )(same, prompt, other, *near, *far)


def resident_kernel(lengths, queries, keys, values, out, top_out, total_out, sums, tops, totals):
    row = pl.program_id(0)
    scores = lax.dot_general(queries[...], keys[0], NT, preferred_element_type=F32)
    scores = scores * HEAD_DIM**-0.5
    slot = lax.broadcasted_iota(jnp.int32, scores.shape, 1)
    scores = jnp.where(slot < lengths[row], scores, LOW)
    top = jnp.max(scores, axis=1, keepdims=True)
    weights = jnp.exp(scores - top)
    total = jnp.sum(weights, axis=1, keepdims=True)
    place = pl.ds(pl.multiple_of(row * GROUPS, GROUPS), GROUPS)
    sums[place, :] = jnp.dot(weights.astype(BF16), values[0], preferred_element_type=F32)
    tops[place, :] = jnp.broadcast_to(top, (GROUPS, HEAD_DIM))
    totals[place, :] = jnp.broadcast_to(total, (GROUPS, HEAD_DIM))

    @pl.when(row == ROWS - 1)
    def _():
        out[...] = sums[...].T
        top_out[...] = tops[...].T[0:8]
        total_out[...] = totals[...].T[0:8]


def resident(lengths, queries, keys, values):
    cache = pl.BlockSpec((1, CONTEXT, HEAD_DIM), lambda i: (i, 0, 0))
    whole = pl.BlockSpec((HEAD_DIM, HEAD_DIM), lambda i: (0, 0))
    stat = pl.BlockSpec((8, HEAD_DIM), lambda i: (0, 0))
    return pl.pallas_call(
        resident_kernel,
        grid=(ROWS,),
        in_specs=[SMEM, pl.BlockSpec((GROUPS, HEAD_DIM), lambda i: (i, 0)), cache, cache],
        out_specs=[whole, stat, stat],
        out_shape=[
            jax.ShapeDtypeStruct((HEAD_DIM, HEAD_DIM), F32),
            jax.ShapeDtypeStruct((8, HEAD_DIM), F32),
            jax.ShapeDtypeStruct((8, HEAD_DIM), F32),
        ],
        scratch_shapes=[pltpu.VMEM((HEAD_DIM, HEAD_DIM), F32)] * 3,
        compiler_params=params(8),
        cost_estimate=cost(4 * ROWS * GROUPS * CONTEXT * HEAD_DIM, 16 * MIB),
        name="resident",
    )(lengths, queries, keys, values)


def split_stats(top, total):
    top_a = top.astype(BF16).astype(F32)
    top_b = (top - top_a).astype(BF16).astype(F32)
    top_c = (top - top_a) - top_b
    total_a = total.astype(BF16).astype(F32)
    total_b = total - total_a
    rows = [top_a, top_b, top_c, total_a, total_b]
    index = lax.broadcasted_iota(jnp.int32, (STAT, HEAD_DIM), 0)
    tile = jnp.zeros((STAT, HEAD_DIM), F32)
    for number, row in enumerate(rows):
        tile = jnp.where(index == number, row, tile)
    return tile.astype(BF16)


def join_stats(tile):
    stats = tile.astype(F32)
    top = (stats[0:1] + stats[1:2]) + stats[2:3]
    return top, stats[3:4] + stats[4:5]


def finish_chunk(parts, cosine, sine, bias, start, key_out, value_out, place):
    count = parts[0].shape[0] - STAT
    squares = jnp.concatenate([part[count:, 0:TILE] for part in parts], axis=0)
    index = lax.broadcasted_iota(jnp.int32, (len(parts) * STAT, HEAD_DIM), 0)
    for tile in range(count // TILE):
        token = slice(tile * TILE, (tile + 1) * TILE)
        table = slice(start + tile * TILE, start + (tile + 1) * TILE)
        target = slice(place + tile * TILE, place + (tile + 1) * TILE)
        chosen = (index % 8) == tile
        total = lax.dot_general(
            squares, jnp.where(chosen, 1.0, 0.0).astype(BF16), TN, preferred_element_type=F32
        )
        inverse = lax.rsqrt(total * (1.0 / D) + 1e-06)
        added = parts[0][token, :].astype(F32)
        for part in parts[1:]:
            added = added + part[token, :].astype(F32)
        keys = added[:, :HEAD_DIM] * inverse + bias[0:1, :]
        values = added[:, HEAD_DIM:] * inverse + bias[1:2, :]
        keys = keys * cosine[table, :] + pltpu.roll(keys, HEAD_DIM // 2, 1) * sine[table, :]
        key_out[target, :] = keys.astype(BF16).astype(F32)
        value_out[target, :] = values.astype(BF16).astype(F32)


def finish_kernel(start, *refs):
    finish_chunk(refs[:4], refs[4], refs[5], refs[6], start, refs[7], refs[8], 0)


def finish(parts, cosine, sine, bias, start):
    count = parts[0].shape[0] - STAT
    return pl.pallas_call(
        functools.partial(finish_kernel, start),
        in_specs=[VMEM] * 7,
        out_specs=[VMEM] * 2,
        out_shape=[jax.ShapeDtypeStruct((count, HEAD_DIM), F32)] * 2,
        compiler_params=params(10),
        cost_estimate=cost(1, 1),
        name="finish",
    )(*parts, cosine, sine, bias)


def attend_kernel(starts, pages, page_rows, place_of, *refs):
    parts, (cosine, sine, bias, near_queries, far_queries) = refs[:4], refs[4:9]
    done = refs[9 : 9 + 2 * (len(starts) - 1)]
    kept, sent, key_store, value_store = refs[9 + len(done) :]
    for number, start in enumerate(starts[:-1]):
        count = done[2 * number].shape[0]
        key_store[start : start + count, :] = done[2 * number][...]
        value_store[start : start + count, :] = done[2 * number + 1][...]
    finish_chunk(parts, cosine, sine, bias, starts[-1], key_store, value_store, starts[-1])

    core = place_of[0]
    lane_row = lax.broadcasted_iota(jnp.int32, (PAGE, HEAD_DIM), 1) // GROUPS

    def attend(replica, query):
        key_pages, value_pages, masks = [], [], []
        for slot in range(SLOTS):
            page = pages[replica * SLOTS + slot]
            place = pl.ds(pl.multiple_of(page * PAGE, PAGE), PAGE)
            key_pages.append(key_store[place, :])
            value_pages.append(value_store[place, :])
            masks.append(lane_row == page_rows[replica * SLOTS + slot])
        keys = jnp.concatenate(key_pages, axis=0).astype(BF16)
        values = jnp.concatenate(value_pages, axis=0).astype(BF16)
        scores = lax.dot_general(keys, query, NT, preferred_element_type=F32)
        scores = scores * HEAD_DIM**-0.5
        scores = jnp.where(jnp.concatenate(masks, axis=0), scores, LOW)
        top = jnp.max(scores, axis=0, keepdims=True)
        weights = jnp.exp(scores - top)
        total = jnp.sum(weights, axis=0, keepdims=True)
        summed = lax.dot_general(values, weights.astype(BF16), TN, preferred_element_type=F32)
        return summed.astype(BF16), split_stats(top, total)

    for flip, queries, out in ((1, far_queries, sent), (0, near_queries, kept)):

        def block(step, carry, flip=flip, queries=queries, out=out):
            for inner in range(8):
                place = step * 8 + inner
                replica = place * 2 + (core + flip) % 2
                summed, stats = attend(replica, queries[place])
                out[place, 0:HEAD_DIM, :] = summed
                out[place, HEAD_DIM : HEAD_DIM + STAT, :] = stats
            return carry

        lax.fori_loop(0, 2, block, 0)


def attend(starts, pages, page_rows, place_of, parts, cosine, sine, bias, near, far, done):
    partial = jax.ShapeDtypeStruct((16, HEAD_DIM + STAT, HEAD_DIM), BF16)
    return pl.pallas_call(
        functools.partial(attend_kernel, starts),
        in_specs=[SMEM] * 3 + [VMEM] * (9 + len(done)),
        out_specs=[VMEM, VMEM],
        out_shape=[partial, partial],
        scratch_shapes=[pltpu.VMEM((TOK, HEAD_DIM), F32)] * 2,
        compiler_params=params(12),
        cost_estimate=cost(1, 1),
        name="attend",
    )(pages, page_rows, place_of, *parts, cosine, sine, bias, near, far, *done)


def merge_kernel(left, right, out):
    def block(step, carry):
        for inner in range(4):
            place = step * 4 + inner
            left_top, left_total = join_stats(left[place, HEAD_DIM:, :])
            right_top, right_total = join_stats(right[place, HEAD_DIM:, :])
            top = jnp.maximum(left_top, right_top)
            left_scale = jnp.exp(left_top - top)
            right_scale = jnp.exp(right_top - top)
            summed = left[place, 0:HEAD_DIM, :].astype(F32) * left_scale
            summed = summed + right[place, 0:HEAD_DIM, :].astype(F32) * right_scale
            out[place, 0:HEAD_DIM, :] = summed.astype(BF16)
            total = left_total * left_scale + right_total * right_scale
            out[place, HEAD_DIM:, :] = split_stats(top, total)
        return carry

    lax.fori_loop(0, 4, block, 0)


def merge(left, right):
    return pl.pallas_call(
        merge_kernel,
        in_specs=[VMEM, VMEM],
        out_specs=VMEM,
        out_shape=jax.ShapeDtypeStruct((16, HEAD_DIM + STAT, HEAD_DIM), BF16),
        compiler_params=params(8),
        cost_estimate=cost(1, 1),
        name="merge",
    )(left, right)


def conclude_kernel(received, sums, tops, totals, out, store):
    stats = [join_stats(received[i, HEAD_DIM:, :]) for i in range(16)]
    top = tops[0:1]
    for part_top, _ in stats:
        top = jnp.maximum(top, part_top)
    scale = jnp.exp(tops[0:1] - top)
    summed = sums[...] * scale
    total = totals[0:1] * scale
    for i, (part_top, part_total) in enumerate(stats):
        scale = jnp.exp(part_top - top)
        summed = summed + received[i, 0:HEAD_DIM, :].astype(F32) * scale
        total = total + part_total * scale
    store[...] = (summed / total).T
    for group in range(GROUPS):
        columns = slice(group * HEAD_DIM, (group + 1) * HEAD_DIM)
        out[:, columns] = store[pl.ds(group, ROWS, stride=GROUPS), :].astype(BF16)


def conclude(received, sums, tops, totals):
    return pl.pallas_call(
        conclude_kernel,
        in_specs=[VMEM] * 4,
        out_specs=VMEM,
        out_shape=jax.ShapeDtypeStruct((ROWS, GROUPS * HEAD_DIM), BF16),
        scratch_shapes=[pltpu.VMEM((HEAD_DIM, HEAD_DIM), F32)],
        compiler_params=params(8),
        cost_estimate=cost(1, 1),
        name="conclude",
    )(received, sums, tops, totals)


def angle_tables(page_offset):
    half = HEAD_DIM // 2
    index = jnp.arange(half, dtype=F32)
    inverse = jnp.exp(-(2.0 * index / HEAD_DIM) * jnp.log(F32(1000000.0)))
    positions = jnp.repeat(page_offset, PAGE) + jnp.tile(
        jnp.arange(PAGE, dtype=jnp.int32), page_offset.shape[0]
    )
    angles = positions.astype(F32)[:, None] * inverse[None, :]
    cosine, sine = jnp.cos(angles), jnp.sin(angles)
    return jnp.concatenate([cosine, cosine], 1), jnp.concatenate([-sine, sine], 1)


def page_tables(page_dest, page_row):
    dest = page_dest[:, 0]
    count = dest.shape[0]
    number = jnp.arange(count, dtype=jnp.int32)
    earlier = (dest[None, :] == dest[:, None]) & (number[None, :] < number[:, None])
    slot = dest * SLOTS + jnp.sum(earlier.astype(jnp.int32), 1)
    match = slot[None, :] == jnp.arange(REPLICAS * SLOTS, dtype=jnp.int32)[:, None]
    pages = jnp.max(jnp.where(match, number[None, :], 0), 1)
    rows = jnp.max(jnp.where(match, page_row[None, :], -1), 1)
    return pages, rows


def per_device(
    prompt,
    norm_gain,
    kv_weight,
    kv_bias,
    page_dest,
    page_row,
    page_offset,
    queries,
    cache_keys,
    cache_values,
    lengths,
):
    tp, rep = lax.axis_index("tp"), lax.axis_index("rep")
    core = rep % 2
    x, y = tp // 2, tp % 2
    starts = [sum(CHUNKS[:i]) for i in range(len(CHUNKS))]

    def rows_of(number, follows=None):
        start, count = starts[number], CHUNKS[number]
        return after(prompt, follows)[start : start + count]

    def swap(rows):
        return permute(rows, lambda x, y, z, h, c: (x, 1 - y, z, h, c))

    def weight_rows(block, follows=None):
        rows = lax.dynamic_slice(
            after(kv_weight, follows), (0, block * FEAT, 0), (2, FEAT, HEAD_DIM)
        )
        gain = lax.dynamic_slice(norm_gain, (block * FEAT,), (FEAT,))
        return (rows.astype(F32) * gain[None, :, None]).astype(BF16)

    def fetch(dx, rows):
        return permute(rows, lambda x, y, z, h, c: ((x + dx) % 4, y, z, h, c))

    def other_core(rows):
        return permute(rows, lambda x, y, z, h, c: (x, y, z, h, 1 - c))

    def wanted(dx, follows):
        return weight_rows(((x + dx) % 4) * 2 + core, follows)

    first_rows = rows_of(0)
    others = [swap(first_rows)]
    one = wanted(1, first_rows)
    three = wanted(3, first_rows)
    two = wanted(2, (one, three))
    near, far = [None] * 4, [None] * 4
    near[1], near[3], near[2] = fetch(1, one), fetch(3, three), fetch(2, two)
    far[2] = other_core(near[2])
    second_rows = rows_of(1, two)
    others.append(swap(second_rows))
    near[0] = weight_rows(x * 2 + core, second_rows)
    far[0] = weight_rows(x * 2 + 1 - core, second_rows)
    cosine, sine = angle_tables(after(page_offset, second_rows))
    query_heads = after(queries, (near[0], far[0], cosine, sine))
    query_heads = query_heads.reshape(ROWS * GROUPS, HEAD_DIM)
    groups = [[zy * 2 + c for zy in range(16)] for c in range(2)]
    near_queries = lax.all_to_all(
        jnp.broadcast_to(query_heads, (16, ROWS * GROUPS, HEAD_DIM)),
        "rep", 0, 0, tiled=True, axis_index_groups=groups,
    )
    far[1], far[3] = other_core(near[1]), other_core(near[3])

    same = (y == core).astype(jnp.int32).reshape(1)
    bias = kv_bias.astype(F32)

    sums, tops, totals = resident(lengths, query_heads, cache_keys, cache_values)
    pages, page_rows = page_tables(page_dest, page_row)

    done = []
    for start, other in zip(starts, others):
        outs = project(same, prompt, start, other, near, far)
        if done:
            outs, done = lax.optimization_barrier((outs, done))
        parts = [outs[0]] + [
            permute(outs[dx], lambda x, y, z, h, c, dx=dx: ((x - dx) % 4, y, z, h, c))
            for dx in (1, 2, 3)
        ]
        if start != starts[-1]:
            done.extend(finish(parts, cosine, sine, bias, start))
    far_queries = other_core(after(near_queries, outs[0]))

    place_of = core.reshape(1)
    kept, sent = attend(
        starts, pages, page_rows, place_of, parts, cosine, sine, bias, near_queries, far_queries, done
    )
    arrived = other_core(sent)
    merged = merge(kept, arrived)
    received = lax.all_to_all(merged, "rep", 0, 0, tiled=True, axis_index_groups=groups)
    return conclude(received, sums, tops, totals)


def solution(mesh):
    placed = (
        P("rep", "tp"),
        P(),
        P(None, None, "tp"),
        P(None, "tp"),
        P("rep", None),
        P("rep"),
        P("rep"),
        P("rep", "tp"),
        P("rep", None, "tp"),
        P("rep", None, "tp"),
        P("rep"),
    )
    return jax.shard_map(
        per_device, mesh=mesh, in_specs=placed, out_specs=P("rep", "tp"), check_vma=False
    )
```
